32 devices in a mesh: group: 2 (over x), row: 16 (over z, y, core).
Axes of the slice: x: 2, y: 2, z: 4, core: 2. Of those that a mesh axis runs over, the one named last changes fastest.
Arguments:
- near_tiles: bfloat16 [2, 5, 1024, 1024], replicated, may hold values from -0.1875 to 0.1875
- near_order: int32 [5], replicated, may hold values from 0 to 4, each once
- receiver_basis: bfloat16 [2, 1024, 16], replicated, may hold values from -1.5 to 1.5
- source_basis: bfloat16 [2, 1024, 16], replicated, may hold values from -0.1875 to 0.1875
- coupling: float32 [2, 16, 16, 16], replicated, may hold values from -0.375 to 0.375
- initial_model: bfloat16 [2, 128, 16384], P(None, 'group', 'row'), parts along dimension 1, may hold values from -6 to 6
- observed: bfloat16 [128, 16384], P('group', 'row'), parts along dimension 0, may hold values from -18 to 18
Outputs:
- model_out: float32 [2, 128, 16384], P(None, 'group', 'row'), parts along dimension 1
- misfit: float32 [128, 16384], P('group', 'row'), parts along dimension 0
The draws below stay inside these ranges and needn't reach their ends.
There are 2 independent parts, one for each index of `group`. The reference program is written for one: setup_inputs(seed, part) draws one part's arguments, and reference() takes and returns one part's arrays. A program takes and returns all parts, laid end to end along the dimension named above; an argument that names none is the same for every part. Nothing has to cross between parts.
Inputs may be any that keep to these rules, and one draw needn't show every extreme that they name: `near_order`: a permutation of 0 to 4.
All inputs are finite; a program needn't handle non-finite values.
Results may differ from the reference program's by a relative error of at most 0.0029.
Values may be sent and summed in bfloat16 or wider, within the bound.
A program may use at most 128 MiB of HBM per device.

```python
import jax
import jax.numpy as jnp
from jax import lax

PTS_DEV = 1024
PERTS = 64
LAYERS = 2
RANK = 16
RADIUS = 2
ITERS = 3
SPAN = 5
POINTS = 16384
N_ROW = 16


def shard_levels(key, dims, pieces, smallest, largest):
    level = 1.0
    for axis_at, parts in pieces:
        heights = jax.random.uniform(jax.random.fold_in(jax.random.fold_in(key, 6), axis_at), (parts,), jnp.float32, smallest / len(pieces), largest / len(pieces))
        level = level * jnp.repeat(jnp.exp(heights), dims[axis_at] // parts).reshape((-1,) + (1,) * (len(dims) - 1 - axis_at))
    return level


def normal_values(own_key, dims, scale, bound, cuts=(), kind=jnp.bfloat16):
    gain = shard_levels(own_key, dims, cuts, -0.22, 0.18) if cuts else 1.0
    values = jax.random.normal(own_key, dims, jnp.float32) * scale * gain
    return jnp.minimum(jnp.maximum(values, -bound), bound).astype(kind)


def setup_inputs(seed: int = 0, part: int = 0) -> dict:
    streams_of = jax.random.split(jax.random.key(seed), 8)
    part_keys = jax.random.split(jax.random.fold_in(streams_of[7], part), 8)
    near_tiles = normal_values(streams_of[0], (LAYERS, SPAN, PTS_DEV, PTS_DEV), PTS_DEV ** -0.5, 0.1875)
    near_order = jax.random.permutation(streams_of[1], SPAN).astype(jnp.int32)
    receiver_basis = normal_values(streams_of[2], (LAYERS, PTS_DEV, RANK), RANK ** -0.5, 1.5)
    source_basis = normal_values(streams_of[3], (LAYERS, PTS_DEV, RANK), PTS_DEV ** -0.5, 0.1875)
    coupling = normal_values(streams_of[4], (LAYERS, N_ROW, RANK, RANK), (RANK * N_ROW) ** -0.5, 0.375, (), jnp.float32)
    initial_model = normal_values(part_keys[5], (LAYERS, PERTS, POINTS), 1.0, 6.0, ((2, 16),))
    observed = normal_values(part_keys[6], (PERTS, POINTS), 3.0, 18.0, ((1, 16),))
    return {"near_tiles": near_tiles, "near_order": near_order, "receiver_basis": receiver_basis, "source_basis": source_basis, "coupling": coupling, "initial_model": initial_model, "observed": observed}


def rounded(values):
    return lax.optimization_barrier(values.astype(jnp.bfloat16)).astype(jnp.float32)


def reference(near_tiles, near_order, receiver_basis, source_basis, coupling, initial_model, observed):
    highest = lax.Precision.HIGHEST
    band_count = N_ROW
    inverse = jnp.argsort(near_order).astype(jnp.int32)
    tile_list = [near_tiles[:, inverse[offset_slot]].astype(jnp.float32) for offset_slot in range(SPAN)]
    band_offsets = jnp.arange(band_count, dtype=jnp.int32)
    far_core = coupling
    position = (band_offsets[:, None] - band_offsets[None, :]) % band_count
    chosen = far_core[:, position]
    receiver_full = receiver_basis.astype(jnp.float32)
    source_full = source_basis.astype(jnp.float32)
    model = initial_model.astype(jnp.float32).reshape(LAYERS, PERTS, band_count, PTS_DEV)
    measured = observed.astype(jnp.float32).reshape(PERTS, band_count, PTS_DEV)
    misfit = measured
    for step_index in range(ITERS):
        model_wire = rounded(model)
        predicted = jnp.zeros((PERTS, band_count, PTS_DEV), jnp.float32)
        for offset_slot in range(SPAN):
            shift_by = offset_slot - RADIUS
            moved = jnp.roll(model_wire, shift_by, axis=2)
            predicted = predicted + jnp.einsum('lpnc,lac->pna', moved, tile_list[offset_slot], precision=highest)
        summary = jnp.einsum('lpnc,lcs->lnsp', model_wire, source_full, precision=highest)
        far_field = jnp.einsum('lijrs,ljsp->lirp', chosen, summary, precision=highest)
        predicted = predicted + jnp.einsum('lar,lirp->pia', receiver_full, far_field, precision=highest)
        misfit = measured - predicted
        misfit_wire = rounded(misfit)
        gradient = jnp.zeros_like(model)
        for offset_slot in range(SPAN):
            shift_by = offset_slot - RADIUS
            moved = jnp.roll(misfit_wire, -shift_by, axis=1)
            gradient = gradient + jnp.einsum('pna,lac->lpnc', moved, tile_list[offset_slot], precision=highest)
        data_summary = jnp.einsum('lar,pia->lirp', receiver_full, misfit_wire, precision=highest)
        far_back = jnp.einsum('lijrs,lirp->ljsp', chosen, data_summary, precision=highest)
        gradient = gradient + jnp.einsum('lcs,ljsp->lpjc', source_full, far_back, precision=highest)
        model = model + 0.01 * (gradient - 10.0 * model)
    return model.reshape(LAYERS, PERTS, band_count * PTS_DEV), misfit.reshape(PERTS, band_count * PTS_DEV)
```

```python
import functools

import jax
import jax.numpy as jnp
from jax import lax
from jax.experimental import pallas as pl
from jax.experimental.pallas import tpu as pltpu
from jax.sharding import PartitionSpec as P

RADIUS = 2
ITERS = 3
CHUNK = 512
HANDED, FAR, PARTNER, NEXT = range(4)
NT = (((1,), (1,)), ((), ()))
NN = (((1,), (0,)), ((), ()))


def mm(lhs, rhs, dims=NN):
    return lax.dot_general(lhs, rhs, dims, preferred_element_type=jnp.float32)


def kernel(
    n, order_ref, tiles_hbm, basis_ref, core_ref, initial_hbm, observed_hbm, model_ref, misfit_ref,
    tiles, initial_ref, observed_ref, initial_in, base, wire_cols, change_cols, misfit_wire,
    part_out, part_in, misfit_in, sent_part, held, arrived, near, sum_f, sum_b,
    tile_sem, small_sem, initial_send, initial_recv, gather_send, gather_recv, halo_send, halo_recv,
):
    layers, perts, points = model_ref.shape
    rank = sum_f.shape[1]
    lr = layers * rank
    me = lax.axis_index("row")
    out = 2 * lax.rem(me, 2) - 1
    small = [
        pltpu.make_async_copy(initial_hbm, initial_ref, small_sem.at[0]),
        pltpu.make_async_copy(observed_hbm, observed_ref, small_sem.at[1]),
    ]
    for load in small:
        load.start()
    loads = [
        pltpu.make_async_copy(tiles_hbm.at[l, k], tiles.at[l, k], tile_sem.at[l, k])
        for l in range(layers)
        for k in range(tiles.shape[1])
    ]
    for load in loads:
        load.start()

    barrier = pltpu.get_barrier_semaphore()

    def greet(d, carry):
        pl.semaphore_signal(
            barrier, inc=1, device_id={"row": lax.rem(me + d, n)}, device_id_type=pl.DeviceIdType.MESH
        )
        return carry

    lax.fori_loop(1, n, greet, 0)
    pl.semaphore_wait(barrier, n - 1)

    slot_of = []
    for o in range(-RADIUS, RADIUS + 1):
        found = jnp.int32(0)
        for k in range(2 * RADIUS + 1):
            found = jnp.maximum(found, jnp.where(order_ref[k] == o + RADIUS, k, 0))
        slot_of.append(found)

    def tile_slot(steps):
        return jnp.where(out > 0, slot_of[RADIUS + steps], slot_of[RADIUS - steps])

    row = lax.broadcasted_iota(jnp.int32, (lr, layers * perts), 0)
    lane = lax.broadcasted_iota(jnp.int32, (lr, layers * perts), 1)
    same_layer = (row // rank) == (lane // perts)

    def pick(full):
        kept = jnp.where(same_layer, full, 0.0)
        return sum(kept[l * rank : (l + 1) * rank] for l in range(layers))

    def gather_copy(buf, which, d, sign):
        return pltpu.make_async_remote_copy(
            src_ref=buf.at[0],
            dst_ref=buf.at[d],
            send_sem=gather_send.at[which],
            recv_sem=gather_recv.at[which],
            device_id={"row": lax.rem(me + sign * d + n, n)},
            device_id_type=pl.DeviceIdType.MESH,
        )

    def gather_start(buf, which, sign):
        def send(d, carry):
            gather_copy(buf, which, d, sign).start()
            return carry

        lax.fori_loop(1, n, send, 0)

    def gather_all(buf, which):
        return pltpu.make_async_remote_copy(
            src_ref=buf.at[pl.ds(1, n - 1)],
            dst_ref=buf.at[pl.ds(1, n - 1)],
            send_sem=gather_send.at[which],
            recv_sem=gather_recv.at[which],
            device_id={"row": lax.rem(me + 1, n)},
            device_id_type=pl.DeviceIdType.MESH,
        )

    def halo(src, dst, which, at, j, steps):
        return pltpu.make_async_remote_copy(
            src_ref=src,
            dst_ref=dst.at[at, j],
            send_sem=halo_send.at[which, at, j],
            recv_sem=halo_recv.at[which, at, j],
            device_id={"row": lax.rem(me + steps * out + n, n)},
            device_id_type=pl.DeviceIdType.MESH,
        )

    def spread(total, which):
        packed = total.reshape(n * rank, layers * perts)
        both = sum(mm(core_ref[which], part) for part in split(packed))
        return split(jnp.where(same_layer, both[:lr] + both[lr:], 0.0).T)

    def split(value):
        if value.dtype == jnp.bfloat16:
            return (value,)
        high = value.astype(jnp.bfloat16)
        return high, (value - high.astype(jnp.float32)).astype(jnp.bfloat16)

    chunks = points // CHUNK
    columns = [pl.ds(j * CHUNK, CHUNK) for j in range(chunks)]

    def upright(value):
        return value.astype(jnp.float32).T.astype(jnp.bfloat16)

    def forward(cells, steps, j):
        return sum(
            mm(tiles[l, tile_slot(steps), columns[j], :], cells[l]) for l in range(layers)
        ).T

    def initial(src, at, l, steps):
        return pltpu.make_async_remote_copy(
            src_ref=src,
            dst_ref=initial_in.at[at, l],
            send_sem=initial_send.at[at, l],
            recv_sem=initial_recv.at[at, l],
            device_id={"row": lax.rem(me + steps * out + n, n)},
            device_id_type=pl.DeviceIdType.MESH,
        )

    def send_part(at, j, steps, value):
        change = (value - sent_part[at, j]).astype(jnp.bfloat16)
        sent_part[at, j] += change.astype(jnp.float32)
        part_out[at, j] = change
        halo(part_out.at[at, j], part_in, 0, at, j, steps).start()

    def backward(source, at):
        value = jnp.concatenate([source[j] for j in range(chunks)], 1)
        for l in range(layers):
            for cols in columns:
                near[l, :, cols] += mm(value, tiles[l, at, :, cols])

    for load in small:
        load.wait()
    for l in range(layers):
        for at, steps in ((NEXT, 1), (FAR, -2), (PARTNER, -1)):
            initial(initial_ref.at[l], at, l, steps).start()
    model_ref[...] = initial_ref[...].astype(jnp.float32)
    for l in range(layers):
        base[l] = upright(initial_ref[l])
    sent_part[...] = jnp.zeros_like(sent_part)
    held[...] = jnp.zeros_like(held)
    arrived[...] = jnp.zeros_like(arrived)

    def step(index, carry):
        model_wire = model_ref[...].astype(jnp.bfloat16)
        sum_f[0] = pick(mm(basis_ref[1], model_wire.reshape(layers * perts, points), NT))
        gather_start(sum_f, 0, 1)
        for l in range(layers):
            wire_cols[l] = upright(model_wire[l])
            change_cols[l] = wire_cols[l] - base[l]

        @pl.when(index == 0)
        def _():
            for l in range(layers):
                initial(initial_ref.at[l], NEXT, l, 1).wait_recv()
                initial(initial_in.at[NEXT, l], HANDED, l, -1).start()
            for load in loads:
                load.wait()
            for at, steps in ((PARTNER, 1), (NEXT, -1), (FAR, -2), (HANDED, 2)):
                if at != NEXT:
                    for l in range(layers):
                        initial(initial_ref.at[l], at, l, 1).wait_recv()
                cells = [upright(initial_in[at, l]) for l in range(layers)]
                for j in range(chunks):
                    arrived[j] += forward(cells, steps, j)
            for at in (HANDED, FAR, PARTNER, NEXT):
                for l in range(layers):
                    initial(initial_ref.at[l], at, l, 1).wait_send()

        @pl.when(index > 0)
        def _():
            for j in range(chunks):
                send_part(HANDED, j, -1, forward(change_cols, -2, j))
                send_part(FAR, j, 2, forward(change_cols, 2, j))
                send_part(PARTNER, j, -1, forward(change_cols, -1, j))
                beside = forward(change_cols, 1, j)
                halo(part_out.at[HANDED, j], part_in, 0, HANDED, j, -1).wait_recv()
                held[j] += part_in[HANDED, j].astype(jnp.float32)
                send_part(NEXT, j, 1, beside + held[j])

        gather_all(sum_f, 0).wait_recv()
        weights = spread(sum_f[...], 0)
        for j in range(chunks):
            both = sum(mm(part, basis_ref[0, :, columns[j]]) for part in weights)
            predicted = forward(wire_cols, 0, j) + sum(
                both[l * perts : (l + 1) * perts] for l in range(layers)
            )

            @pl.when(index > 0)
            def _():
                total = arrived[j]
                for at, steps in ((PARTNER, -1), (NEXT, 1), (FAR, 2)):
                    halo(part_out.at[at, j], part_in, 0, at, j, steps).wait_recv()
                    total = total + part_in[at, j].astype(jnp.float32)
                arrived[j] = total

            misfit = observed_ref[:, columns[j]].astype(jnp.float32) - (predicted + arrived[j])
            misfit_ref[:, columns[j]] = misfit
            misfit_wire[j] = misfit.astype(jnp.bfloat16)
            for at, steps in ((NEXT, 1), (FAR, -2), (PARTNER, -1)):
                halo(misfit_wire.at[j], misfit_in, 1, at, j, steps).start()

        wire = jnp.concatenate([misfit_wire[j] for j in range(chunks)], 1)
        sum_b[0] = pick(
            mm(basis_ref[0], jnp.concatenate([wire] * layers, 0), NT)
        )
        gather_start(sum_b, 1, -1)
        for l in range(layers):
            for cols in columns:
                near[l, :, cols] = mm(wire, tiles[l, tile_slot(0), :, cols])

        def relay(j):
            halo(misfit_wire.at[j], misfit_in, 1, NEXT, j, 1).wait_recv()
            halo(misfit_in.at[NEXT, j], misfit_in, 1, HANDED, j, -1).start()

        def received(at, steps):
            for j in range(chunks):
                halo(misfit_wire.at[j], misfit_in, 1, at, j, steps).wait_recv()

        for j in range(chunks // 2):
            relay(j)
        received(PARTNER, -1)
        backward(misfit_in.at[PARTNER], tile_slot(-1))
        for j in range(chunks // 2, chunks):
            relay(j)
        backward(misfit_in.at[NEXT], tile_slot(1))
        received(FAR, -2)
        backward(misfit_in.at[FAR], tile_slot(2))
        gather_all(sum_b, 1).wait_recv()
        near[...] += sum(
            mm(part, basis_ref[1]) for part in spread(sum_b[...], 1)
        ).reshape(layers, perts, points)
        received(HANDED, -1)
        backward(misfit_in.at[HANDED], tile_slot(-2))
        model = model_ref[...]
        model_ref[...] = model + 0.01 * (near[...] - 10.0 * model)
        for j in range(chunks):
            for at in (HANDED, FAR, PARTNER, NEXT):
                halo(misfit_wire.at[j], misfit_in, 1, at, j, 1).wait_send()

        @pl.when(index > 0)
        def _():
            for j in range(chunks):
                for at in (HANDED, FAR, PARTNER, NEXT):
                    halo(part_out.at[at, j], part_in, 0, at, j, 1).wait_send()

        gather_all(sum_f, 0).wait_send()
        gather_all(sum_b, 1).wait_send()
        return carry

    lax.fori_loop(0, ITERS, step, 0)


def on_device(
    n, near_tiles, near_order, receiver_basis, source_basis, coupling, initial_model, observed
):
    layers, span, points, _ = near_tiles.shape
    rank = receiver_basis.shape[-1]
    perts = observed.shape[0]
    basis = jnp.stack([receiver_basis, source_basis]).transpose(0, 1, 3, 2)
    basis = basis.reshape(2, layers * rank, points)
    ahead = coupling.transpose(0, 2, 1, 3).reshape(layers * rank, n * rank)
    back = coupling.transpose(0, 3, 1, 2).reshape(layers * rank, n * rank)
    core = jnp.stack([ahead, back])
    high = lax.reduce_precision(core, 8, 7)
    core = jnp.concatenate([high, core - high], 1).astype(jnp.bfloat16)
    vmem = pl.BlockSpec(memory_space=pltpu.VMEM)
    chunks = points // CHUNK
    return pl.pallas_call(
        functools.partial(kernel, n),
        out_shape=(
            jax.ShapeDtypeStruct((layers, perts, points), jnp.float32),
            jax.ShapeDtypeStruct((perts, points), jnp.float32),
        ),
        in_specs=[
            pl.BlockSpec(memory_space=pltpu.SMEM),
            pl.BlockSpec(memory_space=pltpu.HBM),
            vmem,
            vmem,
            pl.BlockSpec(memory_space=pltpu.HBM),
            pl.BlockSpec(memory_space=pltpu.HBM),
        ],
        out_specs=(vmem, vmem),
        scratch_shapes=[
            pltpu.VMEM(near_tiles.shape, jnp.bfloat16),
            pltpu.VMEM((layers, perts, points), jnp.bfloat16),
            pltpu.VMEM((perts, points), jnp.bfloat16),
            pltpu.VMEM((4, layers, perts, points), jnp.bfloat16),
            pltpu.VMEM((layers, points, perts), jnp.bfloat16),
            pltpu.VMEM((layers, points, perts), jnp.bfloat16),
            pltpu.VMEM((layers, points, perts), jnp.bfloat16),
            pltpu.VMEM((chunks, perts, CHUNK), jnp.bfloat16),
            pltpu.VMEM((4, chunks, perts, CHUNK), jnp.bfloat16),
            pltpu.VMEM((4, chunks, perts, CHUNK), jnp.bfloat16),
            pltpu.VMEM((4, chunks, perts, CHUNK), jnp.bfloat16),
            pltpu.VMEM((4, chunks, perts, CHUNK), jnp.float32),
            pltpu.VMEM((chunks, perts, CHUNK), jnp.float32),
            pltpu.VMEM((chunks, perts, CHUNK), jnp.float32),
            pltpu.VMEM((layers, perts, points), jnp.float32),
            pltpu.VMEM((n, rank, layers * perts), jnp.float32),
            pltpu.VMEM((n, rank, layers * perts), jnp.float32),
            pltpu.SemaphoreType.DMA((layers, span)),
            pltpu.SemaphoreType.DMA((2,)),
            pltpu.SemaphoreType.DMA((4, layers)),
            pltpu.SemaphoreType.DMA((4, layers)),
            pltpu.SemaphoreType.DMA((2,)),
            pltpu.SemaphoreType.DMA((2,)),
            pltpu.SemaphoreType.DMA((2, 4, chunks)),
            pltpu.SemaphoreType.DMA((2, 4, chunks)),
        ],
        compiler_params=pltpu.CompilerParams(
            collective_id=0, has_side_effects=True, vmem_limit_bytes=63 * 2**20
        ),
    )(near_order, near_tiles, basis, core, initial_model, observed)


def solution(mesh):
    placed = (P(), P(), P(), P(), P(), P(None, "group", "row"), P("group", "row"))
    return jax.shard_map(
        functools.partial(on_device, mesh.shape["row"]),
        mesh=mesh,
        in_specs=placed,
        out_specs=(P(None, "group", "row"), P("group", "row")),
        check_vma=False,
    )
```

```python
import functools

import jax
import jax.numpy as jnp
from jax import lax
from jax.experimental import pallas as pl
from jax.experimental.pallas import tpu as pltpu
from jax.sharding import PartitionSpec as P

RADIUS = 2
ITERS = 3
CHUNK = 512
HANDED, FAR, PARTNER, NEXT = range(4)
NT = (((1,), (1,)), ((), ()))
NN = (((1,), (0,)), ((), ()))


def mm(lhs, rhs, dims=NN):
    return lax.dot_general(lhs, rhs, dims, preferred_element_type=jnp.float32)


def kernel(
    n, order_ref, tiles_hbm, receiver_hbm, source_hbm, coupling_hbm, initial_hbm, observed_hbm,
    model_ref, misfit_ref, tiles, basis_in, coupling_in, core_ref, initial_ref, observed_ref, initial_in, wire, change, misfit_wire,
    part_out, part_in, misfit_in, sent_part, held, arrived, near, sum_f, sum_b,
    tile_sem, small_sem, initial_send, initial_recv, gather_send, gather_recv, halo_send, halo_recv,
):
    layers, perts, points = model_ref.shape
    rank = sum_f.shape[1]
    lr = layers * rank
    me = lax.axis_index("row")
    out = 2 * lax.rem(me, 2) - 1
    small = [
        pltpu.make_async_copy(initial_hbm, initial_ref, small_sem.at[0]),
        pltpu.make_async_copy(observed_hbm, observed_ref, small_sem.at[1]),
        pltpu.make_async_copy(receiver_hbm, basis_in.at[0], small_sem.at[2]),
        pltpu.make_async_copy(source_hbm, basis_in.at[1], small_sem.at[3]),
        pltpu.make_async_copy(coupling_hbm, coupling_in, small_sem.at[4]),
    ]
    for load in small:
        load.start()
    loads = [
        pltpu.make_async_copy(tiles_hbm.at[l, k], tiles.at[l, k], tile_sem.at[l, k])
        for l in range(layers)
        for k in range(tiles.shape[1])
    ]
    for load in loads:
        load.start()

    barrier = pltpu.get_barrier_semaphore()

    def greet(d, carry):
        pl.semaphore_signal(
            barrier, inc=1, device_id={"row": lax.rem(me + d, n)}, device_id_type=pl.DeviceIdType.MESH
        )
        return carry

    lax.fori_loop(1, n, greet, 0)
    pl.semaphore_wait(barrier, n - 1)

    slot_of = []
    for o in range(-RADIUS, RADIUS + 1):
        found = jnp.int32(0)
        for k in range(2 * RADIUS + 1):
            found = jnp.maximum(found, jnp.where(order_ref[k] == o + RADIUS, k, 0))
        slot_of.append(found)

    def tile_slot(steps):
        return jnp.where(out > 0, slot_of[RADIUS + steps], slot_of[RADIUS - steps])

    row = lax.broadcasted_iota(jnp.int32, (lr, layers * perts), 0)
    lane = lax.broadcasted_iota(jnp.int32, (lr, layers * perts), 1)
    same_layer = (row // rank) == (lane // perts)

    def basis(side):
        return basis_in[side].reshape(lr, points)

    def pick(full):
        kept = jnp.where(same_layer, full, 0.0)
        return sum(kept[l * rank : (l + 1) * rank] for l in range(layers))

    def gather_copy(buf, which, d, sign):
        return pltpu.make_async_remote_copy(
            src_ref=buf.at[0],
            dst_ref=buf.at[d],
            send_sem=gather_send.at[which],
            recv_sem=gather_recv.at[which],
            device_id={"row": lax.rem(me + sign * d + n, n)},
            device_id_type=pl.DeviceIdType.MESH,
        )

    def gather_start(buf, which, sign):
        def send(d, carry):
            gather_copy(buf, which, d, sign).start()
            return carry

        lax.fori_loop(1, n, send, 0)

    def gather_all(buf, which):
        return pltpu.make_async_remote_copy(
            src_ref=buf.at[pl.ds(1, n - 1)],
            dst_ref=buf.at[pl.ds(1, n - 1)],
            send_sem=gather_send.at[which],
            recv_sem=gather_recv.at[which],
            device_id={"row": lax.rem(me + 1, n)},
            device_id_type=pl.DeviceIdType.MESH,
        )

    def halo(src, dst, which, at, j, steps):
        return pltpu.make_async_remote_copy(
            src_ref=src,
            dst_ref=dst.at[at, j],
            send_sem=halo_send.at[which, at, j],
            recv_sem=halo_recv.at[which, at, j],
            device_id={"row": lax.rem(me + steps * out + n, n)},
            device_id_type=pl.DeviceIdType.MESH,
        )

    def spread(total, which):
        packed = total.reshape(n * rank, layers * perts)
        both = sum(mm(core_ref[which], part) for part in split(packed))
        return split(jnp.where(same_layer, both[:lr] + both[lr:], 0.0).T)

    def split(value):
        if value.dtype == jnp.bfloat16:
            return (value,)
        high = value.astype(jnp.bfloat16)
        return high, (value - high.astype(jnp.float32)).astype(jnp.bfloat16)

    chunks = points // CHUNK
    columns = [pl.ds(j * CHUNK, CHUNK) for j in range(chunks)]

    def forward(cells, steps, j):
        return sum(
            mm(cells[l], tiles[l, tile_slot(steps), columns[j], :], NT) for l in range(layers)
        )

    def initial(src, at, l, steps):
        return pltpu.make_async_remote_copy(
            src_ref=src,
            dst_ref=initial_in.at[at, l],
            send_sem=initial_send.at[at, l],
            recv_sem=initial_recv.at[at, l],
            device_id={"row": lax.rem(me + steps * out + n, n)},
            device_id_type=pl.DeviceIdType.MESH,
        )

    def send_part(at, j, steps, value):
        change = (value - sent_part[at, j]).astype(jnp.bfloat16)
        sent_part[at, j] += change.astype(jnp.float32)
        part_out[at, j] = change
        halo(part_out.at[at, j], part_in, 0, at, j, steps).start()

    def backward(source, at):
        value = jnp.concatenate([source[j] for j in range(chunks)], 1)
        for l in range(layers):
            for cols in columns:
                near[l, :, cols] += mm(value, tiles[l, at, :, cols])

    for load in small:
        load.wait()
    for l in range(layers):
        for at, steps in ((NEXT, 1), (FAR, -2), (PARTNER, -1)):
            initial(initial_ref.at[l], at, l, steps).start()
    model_ref[...] = initial_ref[...].astype(jnp.float32)
    for l in range(layers):
        rows = pl.ds(l * rank, rank)
        ahead = jnp.concatenate([coupling_in[l, d] for d in range(n)], 1)
        back = jnp.concatenate([coupling_in[l, d].T for d in range(n)], 1)
        for which, core in enumerate((ahead, back)):
            high, low = split(core)
            core_ref[which, rows, :] = high
            core_ref[which, pl.ds(lr + l * rank, rank), :] = low
    sent_part[...] = jnp.zeros_like(sent_part)
    held[...] = jnp.zeros_like(held)
    arrived[...] = jnp.zeros_like(arrived)

    def step(index, carry):
        model_wire = model_ref[...].astype(jnp.bfloat16)
        sum_f[0] = pick(mm(basis(1), model_wire.reshape(layers * perts, points), NT))
        gather_start(sum_f, 0, 1)
        wire[...] = model_wire
        change[...] = model_wire - initial_ref[...]

        @pl.when(index == 0)
        def _():
            for l in range(layers):
                initial(initial_ref.at[l], NEXT, l, 1).wait_recv()
                initial(initial_in.at[NEXT, l], HANDED, l, -1).start()
            for load in loads:
                load.wait()
            for at, steps in ((PARTNER, 1), (NEXT, -1), (FAR, -2), (HANDED, 2)):
                if at != NEXT:
                    for l in range(layers):
                        initial(initial_ref.at[l], at, l, 1).wait_recv()
                cells = initial_in.at[at]
                for j in range(chunks):
                    arrived[j] += forward(cells, steps, j)
            for at in (HANDED, FAR, PARTNER, NEXT):
                for l in range(layers):
                    initial(initial_ref.at[l], at, l, 1).wait_send()

        @pl.when(index > 0)
        def _():
            for j in range(chunks):
                send_part(HANDED, j, -1, forward(change, -2, j))
                send_part(FAR, j, 2, forward(change, 2, j))
                send_part(PARTNER, j, -1, forward(change, -1, j))
                beside = forward(change, 1, j)
                halo(part_out.at[HANDED, j], part_in, 0, HANDED, j, -1).wait_recv()
                held[j] += part_in[HANDED, j].astype(jnp.float32)
                send_part(NEXT, j, 1, beside + held[j])

        gather_all(sum_f, 0).wait_recv()
        weights = spread(sum_f[...], 0)
        for j in range(chunks):
            both = sum(mm(part, basis(0)[:, j * CHUNK : (j + 1) * CHUNK]) for part in weights)
            predicted = forward(wire, 0, j) + sum(
                both[l * perts : (l + 1) * perts] for l in range(layers)
            )

            @pl.when(index > 0)
            def _():
                total = arrived[j]
                for at, steps in ((PARTNER, -1), (NEXT, 1), (FAR, 2)):
                    halo(part_out.at[at, j], part_in, 0, at, j, steps).wait_recv()
                    total = total + part_in[at, j].astype(jnp.float32)
                arrived[j] = total

            misfit = observed_ref[:, columns[j]].astype(jnp.float32) - (predicted + arrived[j])
            misfit_ref[:, columns[j]] = misfit
            misfit_wire[j] = misfit.astype(jnp.bfloat16)
            for at, steps in ((NEXT, 1), (FAR, -2), (PARTNER, -1)):
                halo(misfit_wire.at[j], misfit_in, 1, at, j, steps).start()

        data = jnp.concatenate([misfit_wire[j] for j in range(chunks)], 1)
        sum_b[0] = pick(
            mm(basis(0), jnp.concatenate([data] * layers, 0), NT)
        )
        gather_start(sum_b, 1, -1)
        for l in range(layers):
            for cols in columns:
                near[l, :, cols] = mm(data, tiles[l, tile_slot(0), :, cols])

        def relay(j):
            halo(misfit_wire.at[j], misfit_in, 1, NEXT, j, 1).wait_recv()
            halo(misfit_in.at[NEXT, j], misfit_in, 1, HANDED, j, -1).start()

        def received(at, steps):
            for j in range(chunks):
                halo(misfit_wire.at[j], misfit_in, 1, at, j, steps).wait_recv()

        for j in range(chunks // 2):
            relay(j)
        received(PARTNER, -1)
        backward(misfit_in.at[PARTNER], tile_slot(-1))
        for j in range(chunks // 2, chunks):
            relay(j)
        backward(misfit_in.at[NEXT], tile_slot(1))
        received(FAR, -2)
        backward(misfit_in.at[FAR], tile_slot(2))
        gather_all(sum_b, 1).wait_recv()
        near[...] += sum(
            mm(part, basis(1)) for part in spread(sum_b[...], 1)
        ).reshape(layers, perts, points)
        received(HANDED, -1)
        backward(misfit_in.at[HANDED], tile_slot(-2))
        model = model_ref[...]
        model_ref[...] = model + 0.01 * (near[...] - 10.0 * model)
        for j in range(chunks):
            for at in (HANDED, FAR, PARTNER, NEXT):
                halo(misfit_wire.at[j], misfit_in, 1, at, j, 1).wait_send()

        @pl.when(index > 0)
        def _():
            for j in range(chunks):
                for at in (HANDED, FAR, PARTNER, NEXT):
                    halo(part_out.at[at, j], part_in, 0, at, j, 1).wait_send()

        gather_all(sum_f, 0).wait_send()
        gather_all(sum_b, 1).wait_send()
        return carry

    lax.fori_loop(0, ITERS, step, 0)


def on_device(
    n, near_tiles, near_order, receiver_basis, source_basis, coupling, initial_model, observed
):
    layers, span, points, _ = near_tiles.shape
    rank = receiver_basis.shape[-1]
    perts = observed.shape[0]
    vmem = pl.BlockSpec(memory_space=pltpu.VMEM)
    chunks = points // CHUNK
    fixed = [
        pltpu.with_memory_space_constraint(value, pltpu.HBM)
        for value in (
            receiver_basis.transpose(0, 2, 1), source_basis.transpose(0, 2, 1), coupling, initial_model, observed,
        )
    ]
    return pl.pallas_call(
        functools.partial(kernel, n),
        out_shape=(
            jax.ShapeDtypeStruct((layers, perts, points), jnp.float32),
            jax.ShapeDtypeStruct((perts, points), jnp.float32),
        ),
        in_specs=[
            pl.BlockSpec(memory_space=pltpu.SMEM),
            *[pl.BlockSpec(memory_space=pltpu.HBM)] * 6,
        ],
        out_specs=(vmem, vmem),
        scratch_shapes=[
            pltpu.VMEM(near_tiles.shape, jnp.bfloat16),
            pltpu.VMEM((2, layers, rank, points), jnp.bfloat16),
            pltpu.VMEM(coupling.shape, jnp.float32),
            pltpu.VMEM((2, 2 * layers * rank, n * rank), jnp.bfloat16),
            pltpu.VMEM((layers, perts, points), jnp.bfloat16),
            pltpu.VMEM((perts, points), jnp.bfloat16),
            pltpu.VMEM((4, layers, perts, points), jnp.bfloat16),
            pltpu.VMEM((layers, perts, points), jnp.bfloat16),
            pltpu.VMEM((layers, perts, points), jnp.bfloat16),
            pltpu.VMEM((chunks, perts, CHUNK), jnp.bfloat16),
            pltpu.VMEM((4, chunks, perts, CHUNK), jnp.bfloat16),
            pltpu.VMEM((4, chunks, perts, CHUNK), jnp.bfloat16),
            pltpu.VMEM((4, chunks, perts, CHUNK), jnp.bfloat16),
            pltpu.VMEM((4, chunks, perts, CHUNK), jnp.float32),
            pltpu.VMEM((chunks, perts, CHUNK), jnp.float32),
            pltpu.VMEM((chunks, perts, CHUNK), jnp.float32),
            pltpu.VMEM((layers, perts, points), jnp.float32),
            pltpu.VMEM((n, rank, layers * perts), jnp.float32),
            pltpu.VMEM((n, rank, layers * perts), jnp.float32),
            pltpu.SemaphoreType.DMA((layers, span)),
            pltpu.SemaphoreType.DMA((5,)),
            pltpu.SemaphoreType.DMA((4, layers)),
            pltpu.SemaphoreType.DMA((4, layers)),
            pltpu.SemaphoreType.DMA((2,)),
            pltpu.SemaphoreType.DMA((2,)),
            pltpu.SemaphoreType.DMA((2, 4, chunks)),
            pltpu.SemaphoreType.DMA((2, 4, chunks)),
        ],
        compiler_params=pltpu.CompilerParams(
            collective_id=0, has_side_effects=True, vmem_limit_bytes=52 * 2**20
        ),
    )(
        near_order, near_tiles, *fixed
    )


def solution(mesh):
    placed = (P(), P(), P(), P(), P(), P(None, "group", "row"), P("group", "row"))
    return jax.shard_map(
        functools.partial(on_device, mesh.shape["row"]),
        mesh=mesh,
        in_specs=placed,
        out_specs=(P(None, "group", "row"), P("group", "row")),
        check_vma=False,
    )
```

```python
import functools

import jax
import jax.numpy as jnp
from jax import lax
from jax.experimental import pallas as pl
from jax.experimental.pallas import tpu as pltpu
from jax.sharding import PartitionSpec as P

RADIUS = 2
ITERS = 3
CHUNK = 512
HANDED, FAR, PARTNER, NEXT = range(4)
NT = (((1,), (1,)), ((), ()))
NN = (((1,), (0,)), ((), ()))


def mm(lhs, rhs, dims=NN):
    return lax.dot_general(lhs, rhs, dims, preferred_element_type=jnp.float32)


def kernel(
    n, order_ref, tiles_hbm, receiver_hbm, source_hbm, coupling_hbm, initial_hbm, observed_hbm,
    model_ref, misfit_ref, tiles, basis_in, coupling_in, core_ref, initial_ref, observed_ref, initial_in, wire, change, misfit_wire,
    part_out, part_in, misfit_in, sent_part, held, arrived, near, sum_f, sum_b,
    tile_sem, small_sem, initial_send, initial_recv, gather_send, gather_recv, halo_send, halo_recv,
):
    layers, perts, points = model_ref.shape
    rank = sum_f.shape[1]
    lr = layers * rank
    me = lax.axis_index("row")
    out = 2 * lax.rem(me, 2) - 1
    small = [
        pltpu.make_async_copy(initial_hbm, initial_ref, small_sem.at[0]),
        pltpu.make_async_copy(observed_hbm, observed_ref, small_sem.at[1]),
        pltpu.make_async_copy(receiver_hbm, basis_in.at[0], small_sem.at[2]),
        pltpu.make_async_copy(source_hbm, basis_in.at[1], small_sem.at[3]),
        pltpu.make_async_copy(coupling_hbm, coupling_in, small_sem.at[4]),
    ]
    for load in small:
        load.start()
    loads = [
        pltpu.make_async_copy(tiles_hbm.at[l, k], tiles.at[l, k], tile_sem.at[l, k])
        for l in range(layers)
        for k in range(tiles.shape[1])
    ]
    for load in loads:
        load.start()

    barrier = pltpu.get_barrier_semaphore()

    def wrap(band):
        band = jnp.where(band >= n, band - n, band)
        return jnp.where(band < 0, band + n, band)

    def greet(d, carry):
        pl.semaphore_signal(
            barrier, inc=1, device_id={"row": wrap(me + d)}, device_id_type=pl.DeviceIdType.MESH
        )
        return carry

    lax.fori_loop(1, n, greet, 0)
    pl.semaphore_wait(barrier, n - 1)

    slot_of = []
    for o in range(-RADIUS, RADIUS + 1):
        found = jnp.int32(0)
        for k in range(2 * RADIUS + 1):
            found = jnp.maximum(found, jnp.where(order_ref[k] == o + RADIUS, k, 0))
        slot_of.append(found)

    def tile_slot(steps):
        return jnp.where(out > 0, slot_of[RADIUS + steps], slot_of[RADIUS - steps])

    row = lax.broadcasted_iota(jnp.int32, (lr, layers * perts), 0)
    lane = lax.broadcasted_iota(jnp.int32, (lr, layers * perts), 1)
    same_layer = (row // rank) == (lane // perts)

    def basis(side):
        return basis_in[side].reshape(lr, points)

    def pick(full):
        kept = jnp.where(same_layer, full, 0.0)
        return sum(kept[l * rank : (l + 1) * rank] for l in range(layers))

    def gather_copy(buf, which, d, sign):
        return pltpu.make_async_remote_copy(
            src_ref=buf.at[0],
            dst_ref=buf.at[d],
            send_sem=gather_send.at[which],
            recv_sem=gather_recv.at[which],
            device_id={"row": wrap(me + sign * d)},
            device_id_type=pl.DeviceIdType.MESH,
        )

    def gather_start(buf, which, sign):
        def send(d, carry):
            gather_copy(buf, which, d, sign).start()
            return carry

        lax.fori_loop(1, n, send, 0)

    def gather_all(buf, which):
        return pltpu.make_async_remote_copy(
            src_ref=buf.at[pl.ds(1, n - 1)],
            dst_ref=buf.at[pl.ds(1, n - 1)],
            send_sem=gather_send.at[which],
            recv_sem=gather_recv.at[which],
            device_id={"row": wrap(me + 1)},
            device_id_type=pl.DeviceIdType.MESH,
        )

    def halo(src, dst, which, at, j, steps):
        return pltpu.make_async_remote_copy(
            src_ref=src,
            dst_ref=dst.at[at, j],
            send_sem=halo_send.at[which, at, j],
            recv_sem=halo_recv.at[which, at, j],
            device_id={"row": wrap(me + steps * out)},
            device_id_type=pl.DeviceIdType.MESH,
        )

    def spread(total, which):
        packed = total.reshape(n * rank, layers * perts)
        both = sum(mm(core_ref[which], part) for part in split(packed))
        return split(jnp.where(same_layer, both[:lr] + both[lr:], 0.0).T)

    def split(value):
        if value.dtype == jnp.bfloat16:
            return (value,)
        high = value.astype(jnp.bfloat16)
        return high, (value - high.astype(jnp.float32)).astype(jnp.bfloat16)

    chunks = points // CHUNK
    columns = [pl.ds(j * CHUNK, CHUNK) for j in range(chunks)]

    def forward(cells, steps, j):
        return sum(
            mm(cells[l], tiles[l, tile_slot(steps), columns[j], :], NT) for l in range(layers)
        )

    def initial(src, at, l, steps):
        return pltpu.make_async_remote_copy(
            src_ref=src,
            dst_ref=initial_in.at[at, l],
            send_sem=initial_send.at[at, l],
            recv_sem=initial_recv.at[at, l],
            device_id={"row": wrap(me + steps * out)},
            device_id_type=pl.DeviceIdType.MESH,
        )

    def send_part(at, j, steps, value):
        change = (value - sent_part[at, j]).astype(jnp.bfloat16)
        sent_part[at, j] += change.astype(jnp.float32)
        part_out[at, j] = change
        halo(part_out.at[at, j], part_in, 0, at, j, steps).start()

    def backward(source, at):
        value = jnp.concatenate([source[j] for j in range(chunks)], 1)
        for l in range(layers):
            for cols in columns:
                near[l, :, cols] += mm(value, tiles[l, at, :, cols])

    for load in small:
        load.wait()
    for l in range(layers):
        for at, steps in ((NEXT, 1), (PARTNER, -1)):
            initial(initial_ref.at[l], at, l, steps).start()
    for l in range(layers):
        initial(initial_ref.at[l], FAR, l, -2).start()
    model_ref[...] = initial_ref[...].astype(jnp.float32)
    for l in range(layers):
        rows = pl.ds(l * rank, rank)
        ahead = jnp.concatenate([coupling_in[l, d] for d in range(n)], 1)
        back = jnp.concatenate([coupling_in[l, d].T for d in range(n)], 1)
        for which, core in enumerate((ahead, back)):
            high, low = split(core)
            core_ref[which, rows, :] = high
            core_ref[which, pl.ds(lr + l * rank, rank), :] = low
    sent_part[...] = jnp.zeros_like(sent_part)
    held[...] = jnp.zeros_like(held)
    arrived[...] = jnp.zeros_like(arrived)

    def step(index, carry):
        model_wire = model_ref[...].astype(jnp.bfloat16)
        wire[...] = model_wire
        change[...] = model_wire - initial_ref[...]

        def own():
            for j in range(chunks):
                misfit_ref[:, columns[j]] = forward(wire, 0, j)

        def summarize():
            sum_f[0] = pick(mm(basis(1), model_wire.reshape(layers * perts, points), NT))
            gather_start(sum_f, 0, 1)

        @pl.when(index == 0)
        def _():
            summarize()
            for l in range(layers):
                initial(initial_ref.at[l], NEXT, l, 1).wait_recv()
                initial(initial_in.at[NEXT, l], HANDED, l, -1).start()
            for load in loads:
                load.wait()
            for at, steps in ((PARTNER, 1), (NEXT, -1), (HANDED, 2), (FAR, -2)):
                if at == NEXT:
                    own()
                else:
                    for l in range(layers):
                        initial(initial_ref.at[l], at, l, 1).wait_recv()
                cells = initial_in.at[at]
                for j in range(chunks):
                    arrived[j] += forward(cells, steps, j)
            for at in (HANDED, FAR, PARTNER, NEXT):
                for l in range(layers):
                    initial(initial_ref.at[l], at, l, 1).wait_send()

        @pl.when(index > 0)
        def _():
            for j in range(chunks):
                send_part(HANDED, j, -1, forward(change, -2, j))
                send_part(FAR, j, 2, forward(change, 2, j))
                beside = forward(change, 1, j)
                halo(part_out.at[HANDED, j], part_in, 0, HANDED, j, -1).wait_recv()
                held[j] += part_in[HANDED, j].astype(jnp.float32)
                send_part(NEXT, j, 1, beside + held[j])
                send_part(PARTNER, j, -1, forward(change, -1, j))
                if j == 0:
                    summarize()
            own()

        gather_all(sum_f, 0).wait_recv()
        weights = spread(sum_f[...], 0)
        for j in range(chunks):
            both = sum(mm(part, basis(0)[:, j * CHUNK : (j + 1) * CHUNK]) for part in weights)
            predicted = misfit_ref[:, columns[j]] + sum(
                both[l * perts : (l + 1) * perts] for l in range(layers)
            )

            @pl.when(index > 0)
            def _():
                total = arrived[j]
                for at, steps in ((PARTNER, -1), (NEXT, 1), (FAR, 2)):
                    halo(part_out.at[at, j], part_in, 0, at, j, steps).wait_recv()
                    total = total + part_in[at, j].astype(jnp.float32)
                arrived[j] = total

            misfit = observed_ref[:, columns[j]].astype(jnp.float32) - (predicted + arrived[j])
            misfit_ref[:, columns[j]] = misfit
            misfit_wire[j] = misfit.astype(jnp.bfloat16)
            for at, steps in ((NEXT, 1), (PARTNER, -1)):
                halo(misfit_wire.at[j], misfit_in, 1, at, j, steps).start()
        for j in range(chunks):
            halo(misfit_wire.at[j], misfit_in, 1, FAR, j, -2).start()

        data = jnp.concatenate([misfit_wire[j] for j in range(chunks)], 1)
        sum_b[0] = pick(
            mm(basis(0), jnp.concatenate([data] * layers, 0), NT)
        )
        gather_start(sum_b, 1, -1)
        for l in range(layers):
            for cols in columns:
                near[l, :, cols] = mm(data, tiles[l, tile_slot(0), :, cols])

        def relay(j):
            halo(misfit_wire.at[j], misfit_in, 1, NEXT, j, 1).wait_recv()
            halo(misfit_in.at[NEXT, j], misfit_in, 1, HANDED, j, -1).start()

        def received(at, steps):
            for j in range(chunks):
                halo(misfit_wire.at[j], misfit_in, 1, at, j, steps).wait_recv()

        for j in range(chunks // 2):
            relay(j)
        received(PARTNER, -1)
        backward(misfit_in.at[PARTNER], tile_slot(-1))
        for j in range(chunks // 2, chunks):
            relay(j)
        backward(misfit_in.at[NEXT], tile_slot(1))
        received(HANDED, -1)
        backward(misfit_in.at[HANDED], tile_slot(-2))
        gather_all(sum_b, 1).wait_recv()
        near[...] += sum(
            mm(part, basis(1)) for part in spread(sum_b[...], 1)
        ).reshape(layers, perts, points)
        received(FAR, -2)
        backward(misfit_in.at[FAR], tile_slot(2))
        model = model_ref[...]
        model_ref[...] = model + 0.01 * (near[...] - 10.0 * model)
        for j in range(chunks):
            for at in (HANDED, FAR, PARTNER, NEXT):
                halo(misfit_wire.at[j], misfit_in, 1, at, j, 1).wait_send()

        @pl.when(index > 0)
        def _():
            for j in range(chunks):
                for at in (HANDED, FAR, PARTNER, NEXT):
                    halo(part_out.at[at, j], part_in, 0, at, j, 1).wait_send()

        gather_all(sum_f, 0).wait_send()
        gather_all(sum_b, 1).wait_send()
        return carry

    lax.fori_loop(0, ITERS, step, 0)


def on_device(
    n, near_tiles, near_order, receiver_basis, source_basis, coupling, initial_model, observed
):
    layers, span, points, _ = near_tiles.shape
    rank = receiver_basis.shape[-1]
    perts = observed.shape[0]
    vmem = pl.BlockSpec(memory_space=pltpu.VMEM)
    chunks = points // CHUNK
    fixed = [
        pltpu.with_memory_space_constraint(value, pltpu.HBM)
        for value in (
            receiver_basis.transpose(0, 2, 1), source_basis.transpose(0, 2, 1), coupling, initial_model, observed,
        )
    ]
    return pl.pallas_call(
        functools.partial(kernel, n),
        out_shape=(
            jax.ShapeDtypeStruct((layers, perts, points), jnp.float32),
            jax.ShapeDtypeStruct((perts, points), jnp.float32),
        ),
        in_specs=[
            pl.BlockSpec(memory_space=pltpu.SMEM),
            *[pl.BlockSpec(memory_space=pltpu.HBM)] * 6,
        ],
        out_specs=(vmem, vmem),
        scratch_shapes=[
            pltpu.VMEM(near_tiles.shape, jnp.bfloat16),
            pltpu.VMEM((2, layers, rank, points), jnp.bfloat16),
            pltpu.VMEM(coupling.shape, jnp.float32),
            pltpu.VMEM((2, 2 * layers * rank, n * rank), jnp.bfloat16),
            pltpu.VMEM((layers, perts, points), jnp.bfloat16),
            pltpu.VMEM((perts, points), jnp.bfloat16),
            pltpu.VMEM((4, layers, perts, points), jnp.bfloat16),
            pltpu.VMEM((layers, perts, points), jnp.bfloat16),
            pltpu.VMEM((layers, perts, points), jnp.bfloat16),
            pltpu.VMEM((chunks, perts, CHUNK), jnp.bfloat16),
            pltpu.VMEM((4, chunks, perts, CHUNK), jnp.bfloat16),
            pltpu.VMEM((4, chunks, perts, CHUNK), jnp.bfloat16),
            pltpu.VMEM((4, chunks, perts, CHUNK), jnp.bfloat16),
            pltpu.VMEM((4, chunks, perts, CHUNK), jnp.float32),
            pltpu.VMEM((chunks, perts, CHUNK), jnp.float32),
            pltpu.VMEM((chunks, perts, CHUNK), jnp.float32),
            pltpu.VMEM((layers, perts, points), jnp.float32),
            pltpu.VMEM((n, rank, layers * perts), jnp.float32),
            pltpu.VMEM((n, rank, layers * perts), jnp.float32),
            pltpu.SemaphoreType.DMA((layers, span)),
            pltpu.SemaphoreType.DMA((5,)),
            pltpu.SemaphoreType.DMA((4, layers)),
            pltpu.SemaphoreType.DMA((4, layers)),
            pltpu.SemaphoreType.DMA((2,)),
            pltpu.SemaphoreType.DMA((2,)),
            pltpu.SemaphoreType.DMA((2, 4, chunks)),
            pltpu.SemaphoreType.DMA((2, 4, chunks)),
        ],
        compiler_params=pltpu.CompilerParams(
            collective_id=0, has_side_effects=True, vmem_limit_bytes=52 * 2**20
        ),
    )(
        near_order, near_tiles, *fixed
    )


def solution(mesh):
    placed = (P(), P(), P(), P(), P(), P(None, "group", "row"), P("group", "row"))
    return jax.shard_map(
        functools.partial(on_device, mesh.shape["row"]),
        mesh=mesh,
        in_specs=placed,
        out_specs=(P(None, "group", "row"), P("group", "row")),
        check_vma=False,
    )
```

```python
import functools

import jax
import jax.numpy as jnp
from jax import lax
from jax.experimental import pallas as pl
from jax.experimental.pallas import tpu as pltpu
from jax.sharding import PartitionSpec as P

RADIUS = 2
ITERS = 3
CHUNK = 512
HANDED, FAR, PARTNER, NEXT = range(4)
NT = (((1,), (1,)), ((), ()))
NN = (((1,), (0,)), ((), ()))


def mm(lhs, rhs, dims=NN):
    return lax.dot_general(lhs, rhs, dims, preferred_element_type=jnp.float32)


def kernel(
    n, order_ref, tiles_hbm, receiver_hbm, source_hbm, coupling_hbm, initial_hbm, observed_hbm,
    model_ref, misfit_ref, tiles, basis_in, coupling_in, core_ref, initial_ref, observed_ref, initial_in, wire, change, misfit_wire,
    part_out, part_in, misfit_in, sent_part, held, arrived, near, sum_f, sum_b,
    tile_sem, small_sem, initial_send, initial_recv, gather_send, gather_recv, halo_send, halo_recv,
):
    layers, perts, points = model_ref.shape
    rank = sum_f.shape[1]
    lr = layers * rank
    me = lax.axis_index("row")
    out = 2 * lax.rem(me, 2) - 1
    small = [
        pltpu.make_async_copy(initial_hbm, initial_ref, small_sem.at[0]),
        pltpu.make_async_copy(observed_hbm, observed_ref, small_sem.at[1]),
        pltpu.make_async_copy(receiver_hbm, basis_in.at[0], small_sem.at[2]),
        pltpu.make_async_copy(source_hbm, basis_in.at[1], small_sem.at[3]),
        pltpu.make_async_copy(coupling_hbm, coupling_in, small_sem.at[4]),
    ]
    for load in small:
        load.start()
    loads = [
        pltpu.make_async_copy(tiles_hbm.at[l, k], tiles.at[l, k], tile_sem.at[l, k])
        for l in range(layers)
        for k in range(tiles.shape[1])
    ]
    for load in loads:
        load.start()

    barrier = pltpu.get_barrier_semaphore()

    def wrap(band):
        band = jnp.where(band >= n, band - n, band)
        return jnp.where(band < 0, band + n, band)

    def greet(d, carry):
        pl.semaphore_signal(
            barrier, inc=1, device_id={"row": wrap(me + d)}, device_id_type=pl.DeviceIdType.MESH
        )
        return carry

    lax.fori_loop(1, n, greet, 0)
    pl.semaphore_wait(barrier, n - 1)

    slot_of = []
    for o in range(-RADIUS, RADIUS + 1):
        found = jnp.int32(0)
        for k in range(2 * RADIUS + 1):
            found = jnp.maximum(found, jnp.where(order_ref[k] == o + RADIUS, k, 0))
        slot_of.append(found)

    def tile_slot(steps):
        return jnp.where(out > 0, slot_of[RADIUS + steps], slot_of[RADIUS - steps])

    row = lax.broadcasted_iota(jnp.int32, (lr, layers * perts), 0)
    lane = lax.broadcasted_iota(jnp.int32, (lr, layers * perts), 1)
    same_layer = (row // rank) == (lane // perts)

    def basis(side):
        return basis_in[side].reshape(lr, points)

    def pick(full):
        kept = jnp.where(same_layer, full, 0.0)
        return sum(kept[l * rank : (l + 1) * rank] for l in range(layers))

    def gather_copy(buf, which, d, sign):
        return pltpu.make_async_remote_copy(
            src_ref=buf.at[0],
            dst_ref=buf.at[d],
            send_sem=gather_send.at[which],
            recv_sem=gather_recv.at[which],
            device_id={"row": wrap(me + sign * d)},
            device_id_type=pl.DeviceIdType.MESH,
        )

    def gather_start(buf, which, sign):
        def send(d, carry):
            gather_copy(buf, which, d, sign).start()
            return carry

        lax.fori_loop(1, n, send, 0)

    def gather_all(buf, which):
        return pltpu.make_async_remote_copy(
            src_ref=buf.at[pl.ds(1, n - 1)],
            dst_ref=buf.at[pl.ds(1, n - 1)],
            send_sem=gather_send.at[which],
            recv_sem=gather_recv.at[which],
            device_id={"row": wrap(me + 1)},
            device_id_type=pl.DeviceIdType.MESH,
        )

    def halo(src, dst, which, at, j, steps):
        return pltpu.make_async_remote_copy(
            src_ref=src,
            dst_ref=dst.at[at, j],
            send_sem=halo_send.at[which, at, j],
            recv_sem=halo_recv.at[which, at, j],
            device_id={"row": wrap(me + steps * out)},
            device_id_type=pl.DeviceIdType.MESH,
        )

    def spread(total, which):
        packed = total.reshape(n * rank, layers * perts)
        both = sum(mm(core_ref[which], part) for part in split(packed))
        return split(jnp.where(same_layer, both[:lr] + both[lr:], 0.0).T)

    def split(value):
        if value.dtype == jnp.bfloat16:
            return (value,)
        high = value.astype(jnp.bfloat16)
        return high, (value - high.astype(jnp.float32)).astype(jnp.bfloat16)

    chunks = points // CHUNK
    columns = [pl.ds(j * CHUNK, CHUNK) for j in range(chunks)]

    def forward(cells, steps, j):
        return sum(
            mm(cells[l], tiles[l, tile_slot(steps), columns[j], :], NT) for l in range(layers)
        )

    def initial(src, at, l, steps):
        return pltpu.make_async_remote_copy(
            src_ref=src,
            dst_ref=initial_in.at[at, l],
            send_sem=initial_send.at[at, l],
            recv_sem=initial_recv.at[at, l],
            device_id={"row": wrap(me + steps * out)},
            device_id_type=pl.DeviceIdType.MESH,
        )

    def send_part(at, j, steps, value):
        change = (value - sent_part[at, j]).astype(jnp.bfloat16)
        sent_part[at, j] += change.astype(jnp.float32)
        part_out[at, j] = change
        halo(part_out.at[at, j], part_in, 0, at, j, steps).start()

    def backward(source, at):
        value = jnp.concatenate([source[j] for j in range(chunks)], 1)
        for l in range(layers):
            for cols in columns:
                near[l, :, cols] += mm(value, tiles[l, at, :, cols])

    for load in small:
        load.wait()
    for l in range(layers):
        for at, steps in ((NEXT, 1), (FAR, -2), (PARTNER, -1)):
            initial(initial_ref.at[l], at, l, steps).start()
    model_ref[...] = initial_ref[...].astype(jnp.float32)
    for l in range(layers):
        rows = pl.ds(l * rank, rank)
        ahead = jnp.concatenate([coupling_in[l, d] for d in range(n)], 1)
        back = jnp.concatenate([coupling_in[l, d].T for d in range(n)], 1)
        for which, core in enumerate((ahead, back)):
            high, low = split(core)
            core_ref[which, rows, :] = high
            core_ref[which, pl.ds(lr + l * rank, rank), :] = low
    sent_part[...] = jnp.zeros_like(sent_part)
    held[...] = jnp.zeros_like(held)
    arrived[...] = jnp.zeros_like(arrived)

    def step(index, carry):
        model_wire = model_ref[...].astype(jnp.bfloat16)
        wire[...] = model_wire
        change[...] = model_wire - initial_ref[...]

        def own():
            for j in range(chunks):
                misfit_ref[:, columns[j]] = forward(wire, 0, j)

        def summarize():
            sum_f[0] = pick(mm(basis(1), model_wire.reshape(layers * perts, points), NT))
            gather_start(sum_f, 0, 1)

        summarize()

        @pl.when(index == 0)
        def _():
            for l in range(layers):
                initial(initial_ref.at[l], NEXT, l, 1).wait_recv()
                initial(initial_in.at[NEXT, l], HANDED, l, -1).start()
            for load in loads:
                load.wait()
            for at, steps in ((PARTNER, 1), (NEXT, -1), (FAR, -2), (HANDED, 2)):
                if at == NEXT:
                    own()
                else:
                    for l in range(layers):
                        initial(initial_ref.at[l], at, l, 1).wait_recv()
                cells = initial_in.at[at]
                for j in range(chunks):
                    arrived[j] += forward(cells, steps, j)
            for at in (HANDED, FAR, PARTNER, NEXT):
                for l in range(layers):
                    initial(initial_ref.at[l], at, l, 1).wait_send()

        @pl.when(index > 0)
        def _():
            for j in range(chunks):
                send_part(HANDED, j, -1, forward(change, -2, j))
                send_part(FAR, j, 2, forward(change, 2, j))
                beside = forward(change, 1, j)
                halo(part_out.at[HANDED, j], part_in, 0, HANDED, j, -1).wait_recv()
                held[j] += part_in[HANDED, j].astype(jnp.float32)
                send_part(NEXT, j, 1, beside + held[j])
                send_part(PARTNER, j, -1, forward(change, -1, j))
            own()

        gather_all(sum_f, 0).wait_recv()
        weights = spread(sum_f[...], 0)
        for j in range(chunks):
            both = sum(mm(part, basis(0)[:, j * CHUNK : (j + 1) * CHUNK]) for part in weights)
            predicted = misfit_ref[:, columns[j]] + sum(
                both[l * perts : (l + 1) * perts] for l in range(layers)
            )

            @pl.when(index > 0)
            def _():
                total = arrived[j]
                for at, steps in ((PARTNER, -1), (NEXT, 1), (FAR, 2)):
                    halo(part_out.at[at, j], part_in, 0, at, j, steps).wait_recv()
                    total = total + part_in[at, j].astype(jnp.float32)
                arrived[j] = total

            misfit = observed_ref[:, columns[j]].astype(jnp.float32) - (predicted + arrived[j])
            misfit_ref[:, columns[j]] = misfit
            misfit_wire[j] = misfit.astype(jnp.bfloat16)
            for at, steps in ((NEXT, 1), (FAR, -2), (PARTNER, -1)):
                halo(misfit_wire.at[j], misfit_in, 1, at, j, steps).start()

        data = jnp.concatenate([misfit_wire[j] for j in range(chunks)], 1)
        sum_b[0] = pick(
            mm(basis(0), jnp.concatenate([data] * layers, 0), NT)
        ).astype(jnp.bfloat16)
        gather_start(sum_b, 1, -1)
        for l in range(layers):
            for cols in columns:
                near[l, :, cols] = mm(data, tiles[l, tile_slot(0), :, cols])

        def relay(j):
            halo(misfit_wire.at[j], misfit_in, 1, NEXT, j, 1).wait_recv()
            halo(misfit_in.at[NEXT, j], misfit_in, 1, HANDED, j, -1).start()

        def received(at, steps):
            for j in range(chunks):
                halo(misfit_wire.at[j], misfit_in, 1, at, j, steps).wait_recv()

        for j in range(chunks // 2):
            relay(j)
        received(PARTNER, -1)
        backward(misfit_in.at[PARTNER], tile_slot(-1))
        for j in range(chunks // 2, chunks):
            relay(j)
        backward(misfit_in.at[NEXT], tile_slot(1))
        received(FAR, -2)
        backward(misfit_in.at[FAR], tile_slot(2))
        gather_all(sum_b, 1).wait_recv()
        near[...] += sum(
            mm(part, basis(1)) for part in spread(sum_b[...], 1)
        ).reshape(layers, perts, points)
        received(HANDED, -1)
        backward(misfit_in.at[HANDED], tile_slot(-2))
        model = model_ref[...]
        model_ref[...] = model + 0.01 * (near[...] - 10.0 * model)
        for j in range(chunks):
            for at in (HANDED, FAR, PARTNER, NEXT):
                halo(misfit_wire.at[j], misfit_in, 1, at, j, 1).wait_send()

        @pl.when(index > 0)
        def _():
            for j in range(chunks):
                for at in (HANDED, FAR, PARTNER, NEXT):
                    halo(part_out.at[at, j], part_in, 0, at, j, 1).wait_send()

        gather_all(sum_f, 0).wait_send()
        gather_all(sum_b, 1).wait_send()
        return carry

    lax.fori_loop(0, ITERS, step, 0)


def on_device(
    n, near_tiles, near_order, receiver_basis, source_basis, coupling, initial_model, observed
):
    layers, span, points, _ = near_tiles.shape
    rank = receiver_basis.shape[-1]
    perts = observed.shape[0]
    vmem = pl.BlockSpec(memory_space=pltpu.VMEM)
    chunks = points // CHUNK
    fixed = [
        pltpu.with_memory_space_constraint(value, pltpu.HBM)
        for value in (
            receiver_basis.transpose(0, 2, 1), source_basis.transpose(0, 2, 1), coupling, initial_model, observed,
        )
    ]
    return pl.pallas_call(
        functools.partial(kernel, n),
        out_shape=(
            jax.ShapeDtypeStruct((layers, perts, points), jnp.float32),
            jax.ShapeDtypeStruct((perts, points), jnp.float32),
        ),
        in_specs=[
            pl.BlockSpec(memory_space=pltpu.SMEM),
            *[pl.BlockSpec(memory_space=pltpu.HBM)] * 6,
        ],
        out_specs=(vmem, vmem),
        scratch_shapes=[
            pltpu.VMEM(near_tiles.shape, jnp.bfloat16),
            pltpu.VMEM((2, layers, rank, points), jnp.bfloat16),
            pltpu.VMEM(coupling.shape, jnp.float32),
            pltpu.VMEM((2, 2 * layers * rank, n * rank), jnp.bfloat16),
            pltpu.VMEM((layers, perts, points), jnp.bfloat16),
            pltpu.VMEM((perts, points), jnp.bfloat16),
            pltpu.VMEM((4, layers, perts, points), jnp.bfloat16),
            pltpu.VMEM((layers, perts, points), jnp.bfloat16),
            pltpu.VMEM((layers, perts, points), jnp.bfloat16),
            pltpu.VMEM((chunks, perts, CHUNK), jnp.bfloat16),
            pltpu.VMEM((4, chunks, perts, CHUNK), jnp.bfloat16),
            pltpu.VMEM((4, chunks, perts, CHUNK), jnp.bfloat16),
            pltpu.VMEM((4, chunks, perts, CHUNK), jnp.bfloat16),
            pltpu.VMEM((4, chunks, perts, CHUNK), jnp.float32),
            pltpu.VMEM((chunks, perts, CHUNK), jnp.float32),
            pltpu.VMEM((chunks, perts, CHUNK), jnp.float32),
            pltpu.VMEM((layers, perts, points), jnp.float32),
            pltpu.VMEM((n, rank, layers * perts), jnp.float32),
            pltpu.VMEM((n, rank, layers * perts), jnp.bfloat16),
            pltpu.SemaphoreType.DMA((layers, span)),
            pltpu.SemaphoreType.DMA((5,)),
            pltpu.SemaphoreType.DMA((4, layers)),
            pltpu.SemaphoreType.DMA((4, layers)),
            pltpu.SemaphoreType.DMA((2,)),
            pltpu.SemaphoreType.DMA((2,)),
            pltpu.SemaphoreType.DMA((2, 4, chunks)),
            pltpu.SemaphoreType.DMA((2, 4, chunks)),
        ],
        compiler_params=pltpu.CompilerParams(
            collective_id=0, has_side_effects=True, vmem_limit_bytes=52 * 2**20
        ),
    )(
        near_order, near_tiles, *fixed
    )


def solution(mesh):
    placed = (P(), P(), P(), P(), P(), P(None, "group", "row"), P("group", "row"))
    return jax.shard_map(
        functools.partial(on_device, mesh.shape["row"]),
        mesh=mesh,
        in_specs=placed,
        out_specs=(P(None, "group", "row"), P("group", "row")),
        check_vma=False,
    )
```

```python
import functools

import jax
import jax.numpy as jnp
from jax import lax
from jax.experimental import pallas as pl
from jax.experimental.pallas import tpu as pltpu
from jax.sharding import PartitionSpec as P

RADIUS = 2
ITERS = 3
CHUNK = 256
HANDED, FAR, PARTNER, NEXT = range(4)
NT = (((1,), (1,)), ((), ()))
NN = (((1,), (0,)), ((), ()))


def mm(lhs, rhs, dims=NN):
    return lax.dot_general(lhs, rhs, dims, preferred_element_type=jnp.float32)


def kernel(
    n, order_ref, tiles_hbm, receiver_hbm, source_hbm, coupling_hbm, initial_hbm, observed_hbm,
    model_ref, misfit_ref, tiles, basis_in, coupling_in, core_ref, initial_ref, observed_ref, initial_in, wire, change, misfit_wire,
    part_out, part_in, misfit_in, sent_part, held, arrived, near, sum_f, sum_b,
    tile_sem, small_sem, initial_send, initial_recv, gather_send, gather_recv, halo_send, halo_recv,
):
    layers, perts, points = model_ref.shape
    rank = sum_f.shape[1]
    lr = layers * rank
    me = lax.axis_index("row")
    out = 2 * lax.rem(me, 2) - 1
    small = [
        pltpu.make_async_copy(initial_hbm, initial_ref, small_sem.at[0]),
        pltpu.make_async_copy(observed_hbm, observed_ref, small_sem.at[1]),
        pltpu.make_async_copy(receiver_hbm, basis_in.at[0], small_sem.at[2]),
        pltpu.make_async_copy(source_hbm, basis_in.at[1], small_sem.at[3]),
        pltpu.make_async_copy(coupling_hbm, coupling_in, small_sem.at[4]),
    ]
    for load in small:
        load.start()
    loads = [
        pltpu.make_async_copy(tiles_hbm.at[l, k], tiles.at[l, k], tile_sem.at[l, k])
        for l in range(layers)
        for k in range(tiles.shape[1])
    ]
    for load in loads:
        load.start()

    barrier = pltpu.get_barrier_semaphore()

    def wrap(band):
        band = jnp.where(band >= n, band - n, band)
        return jnp.where(band < 0, band + n, band)

    def greet(d, carry):
        pl.semaphore_signal(
            barrier, inc=1, device_id={"row": wrap(me + d)}, device_id_type=pl.DeviceIdType.MESH
        )
        return carry

    lax.fori_loop(1, n, greet, 0)
    pl.semaphore_wait(barrier, n - 1)

    slot_of = []
    for o in range(-RADIUS, RADIUS + 1):
        found = jnp.int32(0)
        for k in range(2 * RADIUS + 1):
            found = jnp.maximum(found, jnp.where(order_ref[k] == o + RADIUS, k, 0))
        slot_of.append(found)

    def tile_slot(steps):
        return jnp.where(out > 0, slot_of[RADIUS + steps], slot_of[RADIUS - steps])

    row = lax.broadcasted_iota(jnp.int32, (lr, layers * perts), 0)
    lane = lax.broadcasted_iota(jnp.int32, (lr, layers * perts), 1)
    same_layer = (row // rank) == (lane // perts)

    def basis(side):
        return basis_in[side].reshape(lr, points)

    def pick(full):
        kept = jnp.where(same_layer, full, 0.0)
        return sum(kept[l * rank : (l + 1) * rank] for l in range(layers))

    def gather_copy(buf, which, d, sign):
        return pltpu.make_async_remote_copy(
            src_ref=buf.at[0],
            dst_ref=buf.at[d],
            send_sem=gather_send.at[which],
            recv_sem=gather_recv.at[which],
            device_id={"row": wrap(me + sign * d)},
            device_id_type=pl.DeviceIdType.MESH,
        )

    def gather_start(buf, which, sign):
        def send(d, carry):
            gather_copy(buf, which, d, sign).start()
            return carry

        lax.fori_loop(1, n, send, 0)

    def gather_all(buf, which):
        return pltpu.make_async_remote_copy(
            src_ref=buf.at[pl.ds(1, n - 1)],
            dst_ref=buf.at[pl.ds(1, n - 1)],
            send_sem=gather_send.at[which],
            recv_sem=gather_recv.at[which],
            device_id={"row": wrap(me + 1)},
            device_id_type=pl.DeviceIdType.MESH,
        )

    def halo(src, dst, which, at, j, steps):
        return pltpu.make_async_remote_copy(
            src_ref=src,
            dst_ref=dst.at[at, j],
            send_sem=halo_send.at[which, at, j],
            recv_sem=halo_recv.at[which, at, j],
            device_id={"row": wrap(me + steps * out)},
            device_id_type=pl.DeviceIdType.MESH,
        )

    def spread(total, which):
        packed = total.reshape(n * rank, layers * perts)
        both = sum(mm(core_ref[which], part) for part in split(packed))
        return split(jnp.where(same_layer, both[:lr] + both[lr:], 0.0).T)

    def split(value):
        if value.dtype == jnp.bfloat16:
            return (value,)
        high = value.astype(jnp.bfloat16)
        return high, (value - high.astype(jnp.float32)).astype(jnp.bfloat16)

    chunks = points // CHUNK
    columns = [pl.ds(j * CHUNK, CHUNK) for j in range(chunks)]

    def forward(cells, steps, j):
        return sum(
            mm(cells[l], tiles[l, tile_slot(steps), columns[j], :], NT) for l in range(layers)
        )

    def initial(src, at, l, steps):
        return pltpu.make_async_remote_copy(
            src_ref=src,
            dst_ref=initial_in.at[at, l],
            send_sem=initial_send.at[at, l],
            recv_sem=initial_recv.at[at, l],
            device_id={"row": wrap(me + steps * out)},
            device_id_type=pl.DeviceIdType.MESH,
        )

    def send_part(at, j, steps, value):
        change = (value - sent_part[at, j]).astype(jnp.bfloat16)
        sent_part[at, j] += change.astype(jnp.float32)
        part_out[at, j] = change
        halo(part_out.at[at, j], part_in, 0, at, j, steps).start()

    def backward(source, at):
        value = jnp.concatenate([source[j] for j in range(chunks)], 1)
        for l in range(layers):
            for cols in columns:
                near[l, :, cols] += mm(value, tiles[l, at, :, cols])

    for load in small:
        load.wait()
    for l in range(layers):
        for at, steps in ((NEXT, 1), (FAR, -2), (PARTNER, -1)):
            initial(initial_ref.at[l], at, l, steps).start()
    model_ref[...] = initial_ref[...].astype(jnp.float32)
    for l in range(layers):
        rows = pl.ds(l * rank, rank)
        ahead = jnp.concatenate([coupling_in[l, d] for d in range(n)], 1)
        back = jnp.concatenate([coupling_in[l, d].T for d in range(n)], 1)
        for which, core in enumerate((ahead, back)):
            high, low = split(core)
            core_ref[which, rows, :] = high
            core_ref[which, pl.ds(lr + l * rank, rank), :] = low
    sent_part[...] = jnp.zeros_like(sent_part)
    held[...] = jnp.zeros_like(held)
    arrived[...] = jnp.zeros_like(arrived)

    def step(index, carry):
        model_wire = model_ref[...].astype(jnp.bfloat16)
        wire[...] = model_wire
        change[...] = model_wire - initial_ref[...]

        def own():
            for j in range(chunks):
                misfit_ref[:, columns[j]] = forward(wire, 0, j)

        def summarize():
            sum_f[0] = pick(mm(basis(1), model_wire.reshape(layers * perts, points), NT))
            gather_start(sum_f, 0, 1)

        summarize()

        @pl.when(index == 0)
        def _():
            for l in range(layers):
                initial(initial_ref.at[l], NEXT, l, 1).wait_recv()
                initial(initial_in.at[NEXT, l], HANDED, l, -1).start()
            for load in loads:
                load.wait()
            for at, steps in ((PARTNER, 1), (NEXT, -1), (FAR, -2), (HANDED, 2)):
                if at == NEXT:
                    own()
                else:
                    for l in range(layers):
                        initial(initial_ref.at[l], at, l, 1).wait_recv()
                cells = initial_in.at[at]
                for j in range(chunks):
                    arrived[j] += forward(cells, steps, j)
            for at in (HANDED, FAR, PARTNER, NEXT):
                for l in range(layers):
                    initial(initial_ref.at[l], at, l, 1).wait_send()

        @pl.when(index > 0)
        def _():
            for j in range(chunks):
                send_part(HANDED, j, -1, forward(change, -2, j))
                send_part(FAR, j, 2, forward(change, 2, j))
                beside = forward(change, 1, j)
                halo(part_out.at[HANDED, j], part_in, 0, HANDED, j, -1).wait_recv()
                held[j] += part_in[HANDED, j].astype(jnp.float32)
                send_part(NEXT, j, 1, beside + held[j])
                send_part(PARTNER, j, -1, forward(change, -1, j))
            own()

        gather_all(sum_f, 0).wait_recv()
        weights = spread(sum_f[...], 0)
        for j in range(chunks):
            both = sum(mm(part, basis(0)[:, j * CHUNK : (j + 1) * CHUNK]) for part in weights)
            predicted = misfit_ref[:, columns[j]] + sum(
                both[l * perts : (l + 1) * perts] for l in range(layers)
            )

            @pl.when(index > 0)
            def _():
                total = arrived[j]
                for at, steps in ((PARTNER, -1), (NEXT, 1), (FAR, 2)):
                    halo(part_out.at[at, j], part_in, 0, at, j, steps).wait_recv()
                    total = total + part_in[at, j].astype(jnp.float32)
                arrived[j] = total

            misfit = observed_ref[:, columns[j]].astype(jnp.float32) - (predicted + arrived[j])
            misfit_ref[:, columns[j]] = misfit
            misfit_wire[j] = misfit.astype(jnp.bfloat16)
            for at, steps in ((NEXT, 1), (FAR, -2), (PARTNER, -1)):
                halo(misfit_wire.at[j], misfit_in, 1, at, j, steps).start()

        data = jnp.concatenate([misfit_wire[j] for j in range(chunks)], 1)
        sum_b[0] = pick(
            mm(basis(0), jnp.concatenate([data] * layers, 0), NT)
        ).astype(jnp.bfloat16)
        gather_start(sum_b, 1, -1)
        for l in range(layers):
            for cols in columns:
                near[l, :, cols] = mm(data, tiles[l, tile_slot(0), :, cols])

        def relay(j):
            halo(misfit_wire.at[j], misfit_in, 1, NEXT, j, 1).wait_recv()
            halo(misfit_in.at[NEXT, j], misfit_in, 1, HANDED, j, -1).start()

        def received(at, steps):
            for j in range(chunks):
                halo(misfit_wire.at[j], misfit_in, 1, at, j, steps).wait_recv()

        for j in range(chunks // 2):
            relay(j)
        received(PARTNER, -1)
        backward(misfit_in.at[PARTNER], tile_slot(-1))
        for j in range(chunks // 2, chunks):
            relay(j)
        backward(misfit_in.at[NEXT], tile_slot(1))
        received(FAR, -2)
        backward(misfit_in.at[FAR], tile_slot(2))
        gather_all(sum_b, 1).wait_recv()
        near[...] += sum(
            mm(part, basis(1)) for part in spread(sum_b[...], 1)
        ).reshape(layers, perts, points)
        received(HANDED, -1)
        backward(misfit_in.at[HANDED], tile_slot(-2))
        model = model_ref[...]
        model_ref[...] = model + 0.01 * (near[...] - 10.0 * model)
        for j in range(chunks):
            for at in (HANDED, FAR, PARTNER, NEXT):
                halo(misfit_wire.at[j], misfit_in, 1, at, j, 1).wait_send()

        @pl.when(index > 0)
        def _():
            for j in range(chunks):
                for at in (HANDED, FAR, PARTNER, NEXT):
                    halo(part_out.at[at, j], part_in, 0, at, j, 1).wait_send()

        gather_all(sum_f, 0).wait_send()
        gather_all(sum_b, 1).wait_send()
        return carry

    lax.fori_loop(0, ITERS, step, 0)


def on_device(
    n, near_tiles, near_order, receiver_basis, source_basis, coupling, initial_model, observed
):
    layers, span, points, _ = near_tiles.shape
    rank = receiver_basis.shape[-1]
    perts = observed.shape[0]
    vmem = pl.BlockSpec(memory_space=pltpu.VMEM)
    chunks = points // CHUNK
    fixed = [
        pltpu.with_memory_space_constraint(value, pltpu.HBM)
        for value in (
            receiver_basis.transpose(0, 2, 1), source_basis.transpose(0, 2, 1), coupling, initial_model, observed,
        )
    ]
    return pl.pallas_call(
        functools.partial(kernel, n),
        out_shape=(
            jax.ShapeDtypeStruct((layers, perts, points), jnp.float32),
            jax.ShapeDtypeStruct((perts, points), jnp.float32),
        ),
        in_specs=[
            pl.BlockSpec(memory_space=pltpu.SMEM),
            *[pl.BlockSpec(memory_space=pltpu.HBM)] * 6,
        ],
        out_specs=(vmem, vmem),
        scratch_shapes=[
            pltpu.VMEM(near_tiles.shape, jnp.bfloat16),
            pltpu.VMEM((2, layers, rank, points), jnp.bfloat16),
            pltpu.VMEM(coupling.shape, jnp.float32),
            pltpu.VMEM((2, 2 * layers * rank, n * rank), jnp.bfloat16),
            pltpu.VMEM((layers, perts, points), jnp.bfloat16),
            pltpu.VMEM((perts, points), jnp.bfloat16),
            pltpu.VMEM((4, layers, perts, points), jnp.bfloat16),
            pltpu.VMEM((layers, perts, points), jnp.bfloat16),
            pltpu.VMEM((layers, perts, points), jnp.bfloat16),
            pltpu.VMEM((chunks, perts, CHUNK), jnp.bfloat16),
            pltpu.VMEM((4, chunks, perts, CHUNK), jnp.bfloat16),
            pltpu.VMEM((4, chunks, perts, CHUNK), jnp.bfloat16),
            pltpu.VMEM((4, chunks, perts, CHUNK), jnp.bfloat16),
            pltpu.VMEM((4, chunks, perts, CHUNK), jnp.float32),
            pltpu.VMEM((chunks, perts, CHUNK), jnp.float32),
            pltpu.VMEM((chunks, perts, CHUNK), jnp.float32),
            pltpu.VMEM((layers, perts, points), jnp.float32),
            pltpu.VMEM((n, rank, layers * perts), jnp.float32),
            pltpu.VMEM((n, rank, layers * perts), jnp.bfloat16),
            pltpu.SemaphoreType.DMA((layers, span)),
            pltpu.SemaphoreType.DMA((5,)),
            pltpu.SemaphoreType.DMA((4, layers)),
            pltpu.SemaphoreType.DMA((4, layers)),
            pltpu.SemaphoreType.DMA((2,)),
            pltpu.SemaphoreType.DMA((2,)),
            pltpu.SemaphoreType.DMA((2, 4, chunks)),
            pltpu.SemaphoreType.DMA((2, 4, chunks)),
        ],
        compiler_params=pltpu.CompilerParams(
            collective_id=0, has_side_effects=True, vmem_limit_bytes=52 * 2**20
        ),
    )(
        near_order, near_tiles, *fixed
    )


def solution(mesh):
    placed = (P(), P(), P(), P(), P(), P(None, "group", "row"), P("group", "row"))
    return jax.shard_map(
        functools.partial(on_device, mesh.shape["row"]),
        mesh=mesh,
        in_specs=placed,
        out_specs=(P(None, "group", "row"), P("group", "row")),
        check_vma=False,
    )
```
